256 devices in a mesh: seq: 32 (over y, x, core), dp: 8 (over z).
Axes of the slice: x: 4, y: 4, z: 8, core: 2. Of those that a mesh axis runs over, the one named last changes fastest.
Arguments:
- cross_queries: bfloat16 [8, 4096, 4096], P('dp', 'seq')
- cross_cotangent: bfloat16 [8, 4096, 4096], P('dp', 'seq'), may hold values from -6 to 6
- gate: float32 [32], replicated, may hold values from -1.5 to 1.5
- vision_kv: bfloat16 [8, 32, 1601, 1024], P('dp', 'seq')
- block_map: int32 [8, 32], P('dp', 'seq'), may hold values from 0 to 2, as said below
- self_queries: bfloat16 [8, 4096, 4096], P('dp', 'seq')
- self_keys: bfloat16 [8, 4096, 512], P('dp', 'seq')
- self_values: bfloat16 [8, 4096, 512], P('dp', 'seq'), may hold values from -6 to 6
- self_cotangent: bfloat16 [8, 4096, 4096], P('dp', 'seq'), may hold values from -6 to 6
- doc_ids: int32 [8, 4096], P('dp', 'seq'), may hold values from 0 to 15, never falling along the last dimension, each value on 1 to 512 neighbouring positions
Outputs:
- cross_query_grad: bfloat16 [8, 4096, 4096], P('dp', 'seq')
- gate_grad: float32 [32], replicated
- vision_grad: bfloat16 [8, 32, 1601, 1024], P('dp', 'seq')
- self_query_grad: bfloat16 [8, 4096, 4096], P('dp', 'seq')
- self_key_grad: bfloat16 [8, 4096, 512], P('dp', 'seq')
- self_value_grad: bfloat16 [8, 4096, 512], P('dp', 'seq')
The draws below stay inside these ranges and needn't reach their ends.
Inputs may be any that keep to these rules, and one draw needn't show every extreme that they name: `block_map`: 0: the span attends its own image block; 1: the block before it; 2: no image. The first span of a sequence never holds 1. `doc_ids`: ids never fall along a sequence; each document holds at most 512 tokens.
All inputs are finite; a program needn't handle non-finite values.
Results may differ from the reference program's by a relative error of at most 0.012.
The reference program's roundings to bfloat16 on the way count: a program that leaves them out, or rounds other values in their place, can miss the bound.
Values may be sent and summed in bfloat16 or wider, within the bound.
A program may use at most 128 MiB of HBM per device.

```python
import math
import jax
import jax.numpy as jnp
import numpy as np
from jax import lax

HEADS = 32
KVH = 4
HD = 128
VROWS = 1601
TOK_DEV = 128
QBLOCK = 256
MOST = 512
SEQS = 8
BLOCKS = 32
TOKENS = 4096
DOCS = 16


def draw_cross_queries(key, part):
    key = jax.random.fold_in(key, 11)
    values = jax.random.normal(key, (SEQS, TOKENS, HEADS * HD), jnp.float32)
    return values.astype(jnp.bfloat16)


def draw_vision_kv(key, part):
    key = jax.random.fold_in(key, 12)
    values = jax.random.normal(key, (SEQS, BLOCKS, VROWS, 2 * KVH * HD), jnp.float32)
    return values.astype(jnp.bfloat16)


def draw_self_queries(key, part):
    key = jax.random.fold_in(key, 13)
    values = jax.random.normal(key, (SEQS, TOKENS, HEADS * HD), jnp.float32)
    return values.astype(jnp.bfloat16)


def draw_self_keys(key, part):
    key = jax.random.fold_in(key, 14)
    values = jax.random.normal(key, (SEQS, TOKENS, KVH * HD), jnp.float32)
    return values.astype(jnp.bfloat16)


def draw_block_map(key, part):
    key = jax.random.fold_in(key, 15)
    chosen = jax.random.randint(key, (SEQS, BLOCKS), 0, 3, jnp.int32)
    first_span = jnp.where(chosen[:, 0] == 1, 0, chosen[:, 0]).astype(jnp.int32)
    return chosen.at[:, 0].set(first_span)


def level_of(own_key, extent, pieces, low, largest):
    level = 1.0
    for position, shards_of in pieces:
        steps = jax.random.uniform(jax.random.fold_in(jax.random.fold_in(own_key, 6), position), (shards_of,), jnp.float32, low / len(pieces), largest / len(pieces))
        level = level * jnp.repeat(jnp.exp(steps), extent[position] // shards_of).reshape((-1,) + (1,) * (len(extent) - 1 - position))
    return level


def length_profile(number_of, total, limit, lean):
    portions = [(1 << 20) // math.isqrt(rank ** lean) + 1 for rank in range(2, number_of + 1)]
    spare, holding = total - limit - (number_of - 1), [1] * (number_of - 1)
    while spare > 0:
        free = [i for i in range(number_of - 1) if holding[i] < limit]
        whole, left = sum([portions[i] for i in free]), spare
        for i in free:
            addition = min(limit - holding[i], max(1, left * portions[i] // whole), spare)
            holding[i] = holding[i] + addition
            spare = spare - addition
    return np.array([limit] + holding)


def ragged_sizes(rng, count, total, limit, skew):
    if count == 2:
        one = jax.random.randint(rng, (), max(1, total - limit), min(limit, total - 1) + 1)
        return jnp.stack([one, total - one])
    tallies = jnp.asarray(length_profile(count, total, limit, skew), jnp.int32)
    pairs = (count - 1) // 2
    giver, receiver = tallies[1:1 + 2 * pairs:2], tallies[2:2 + 2 * pairs:2]
    room = jnp.minimum(giver - 1, limit - receiver)
    passed = jax.random.randint(jax.random.fold_in(rng, 1), (pairs,), 0, 1 << 20) % (room + 1)
    tallies = tallies.at[1:1 + 2 * pairs:2].set(giver - passed).at[2:2 + 2 * pairs:2].set(receiver + passed)
    return tallies[jax.random.permutation(jax.random.fold_in(rng, 2), count)]


def bell_draw(rng, extent, scale, reach, shards=(), kind=jnp.bfloat16):
    gain = level_of(rng, extent, shards, -0.22, 0.18) if shards else 1.0
    drawn = jax.random.normal(rng, extent, jnp.float32) * scale * gain
    return jnp.minimum(jnp.maximum(drawn, -reach), reach).astype(kind)


def setup_inputs(seed: int = 0) -> dict:
    keys = jax.random.split(jax.random.key(seed), 11)
    return {
        "cross_queries": draw_cross_queries(jax.random.fold_in(keys[10], 71), 0),
        "cross_cotangent": bell_draw(keys[1], (SEQS, TOKENS, HEADS * HD), 1.0, 6.0, ((0, 8), (1, 32))),
        "gate": jnp.clip(jax.random.uniform(keys[2], (HEADS,), jnp.float32, -1.5, 1.5), -1.5, 1.5),
        "vision_kv": draw_vision_kv(jax.random.fold_in(keys[10], 71), 0),
        "block_map": draw_block_map(jax.random.fold_in(keys[10], 71), 0),
        "self_queries": draw_self_queries(jax.random.fold_in(keys[10], 71), 0),
        "self_keys": draw_self_keys(jax.random.fold_in(keys[10], 71), 0),
        "self_values": bell_draw(keys[7], (SEQS, TOKENS, KVH * HD), 1.0, 6.0, ((0, 8), (1, 32))),
        "self_cotangent": bell_draw(keys[8], (SEQS, TOKENS, HEADS * HD), 1.0, 6.0, ((0, 8), (1, 32))),
        "doc_ids": jax.vmap(lambda own: jnp.searchsorted(jnp.cumsum(ragged_sizes(own, DOCS, TOKENS, MOST, 0)), jnp.arange(TOKENS), side="right"))(jax.random.split(keys[9], SEQS)).reshape((SEQS, TOKENS)).astype(jnp.int32),
    }


NEG_LARGE = -1.0e30


def to_low(values):
    return lax.optimization_barrier(values.astype(jnp.bfloat16)).astype(jnp.float32)


def cross_span(queries, cotangent, block, gate):
    rows = queries.shape[0]
    group_size = HEADS // KVH
    factor = HD ** -0.5
    tanh_gate = jnp.tanh(gate)
    query_heads = queries.reshape(rows, KVH, group_size, HD).transpose(1, 0, 2, 3)
    cot_heads = cotangent.reshape(rows, KVH, group_size, HD).transpose(1, 0, 2, 3)
    key_heads = block[:, :KVH * HD].reshape(VROWS, KVH, HD).transpose(1, 0, 2)
    value_heads = block[:, KVH * HD:].reshape(VROWS, KVH, HD).transpose(1, 0, 2)
    gate_heads = tanh_gate.reshape(KVH, group_size)

    def one_head(operands):
        query_one, cot_one, key_one, value_one, gate_one = operands
        query_wide = query_one.astype(jnp.float32)
        key_wide = key_one.astype(jnp.float32)
        value_wide = value_one.astype(jnp.float32)
        cot_wide = cot_one.astype(jnp.float32)
        scores = jnp.einsum("rgd,vd->rgv", query_wide, key_wide) * factor
        row_max = jnp.max(scores, axis=-1, keepdims=True)
        weights = jnp.exp(scores - row_max)
        weights = weights / jnp.sum(weights, axis=-1, keepdims=True)
        weights_low = to_low(weights)
        attended = jnp.einsum("rgv,vd->rgd", weights_low, value_wide)
        inner = jnp.sum(cot_wide * attended, axis=-1)
        out_grad = to_low(gate_one[None, :, None] * cot_wide)
        delta = gate_one[None, :] * inner
        weight_grad = jnp.einsum("rgd,vd->rgv", out_grad, value_wide)
        score_grad = to_low(weights * (weight_grad - delta[:, :, None]))
        query_grad = jnp.einsum("rgv,vd->rgd", score_grad, key_wide) * factor
        key_grad = jnp.einsum("rgv,rgd->vd", score_grad, query_wide) * factor
        value_grad = jnp.einsum("rgv,rgd->vd", weights_low, out_grad)
        return query_grad, key_grad, value_grad, jnp.sum(inner, axis=0)

    query_grad, key_grad, value_grad, inner_sum = lax.map(
        one_head, (query_heads, cot_heads, key_heads, value_heads, gate_heads))
    query_grad = query_grad.transpose(1, 0, 2, 3).reshape(rows, HEADS * HD).astype(jnp.bfloat16)
    block_grad = jnp.concatenate(
        [key_grad.transpose(1, 0, 2).reshape(VROWS, KVH * HD),
         value_grad.transpose(1, 0, 2).reshape(VROWS, KVH * HD)], axis=1)
    gate_term = (1.0 - tanh_gate * tanh_gate) * inner_sum.reshape(HEADS)
    return query_grad, block_grad, gate_term


def self_attend(query_heads, key_heads, value_heads, cot_heads, docs):
    all_tokens = query_heads.shape[0]
    factor = HD ** -0.5
    window = QBLOCK + MOST
    query_pos = jnp.arange(QBLOCK, dtype=jnp.int32)
    key_pos = jnp.arange(window, dtype=jnp.int32)

    def step(totals, block_index):
        key_total, value_total = totals
        first_row = (block_index * QBLOCK).astype(jnp.int32)
        key_start = jnp.maximum(first_row - MOST, 0).astype(jnp.int32)
        query_block = lax.dynamic_slice_in_dim(query_heads, first_row, QBLOCK, 0).astype(jnp.float32)
        cot_block = lax.dynamic_slice_in_dim(cot_heads, first_row, QBLOCK, 0).astype(jnp.float32)
        key_window = lax.dynamic_slice_in_dim(key_heads, key_start, window, 0).astype(jnp.float32)
        value_window = lax.dynamic_slice_in_dim(value_heads, key_start, window, 0).astype(jnp.float32)
        query_docs = lax.dynamic_slice_in_dim(docs, first_row, QBLOCK, 0)
        key_docs = lax.dynamic_slice_in_dim(docs, key_start, window, 0)
        allowed = ((key_start + key_pos)[None, :] <= (first_row + query_pos)[:, None]) & (
            key_docs[None, :] == query_docs[:, None])
        scores = jnp.einsum("qhd,khd->hqk", query_block, key_window) * factor
        scores = jnp.where(allowed[None], scores, NEG_LARGE)
        row_max = jnp.max(scores, axis=-1, keepdims=True)
        weights = jnp.exp(scores - row_max)
        weights = weights / jnp.sum(weights, axis=-1, keepdims=True)
        weights_low = to_low(weights)
        attended = jnp.einsum("hqk,khd->qhd", weights_low, value_window)
        delta = jnp.sum(cot_block * attended, axis=-1)
        weight_grad = jnp.einsum("qhd,khd->hqk", cot_block, value_window)
        score_grad = to_low(weights * (weight_grad - delta.T[:, :, None]))
        query_grad = (jnp.einsum("hqk,khd->qhd", score_grad, key_window) * factor).astype(jnp.bfloat16)
        key_grad = jnp.einsum("hqk,qhd->khd", score_grad, query_block) * factor
        value_grad = jnp.einsum("hqk,qhd->khd", weights_low, cot_block)
        key_total = lax.dynamic_update_slice_in_dim(
            key_total, lax.dynamic_slice_in_dim(key_total, key_start, window, 0) + key_grad, key_start, 0)
        value_total = lax.dynamic_update_slice_in_dim(
            value_total, lax.dynamic_slice_in_dim(value_total, key_start, window, 0) + value_grad, key_start, 0)
        return (key_total, value_total), query_grad

    zeros_grad = jnp.zeros(query_heads.shape, jnp.float32)
    block_count = all_tokens // QBLOCK
    (key_total, value_total), query_grad = lax.scan(
        step, (zeros_grad, zeros_grad), jnp.arange(block_count, dtype=jnp.int32))
    return query_grad.reshape(query_heads.shape), key_total, value_total


def reference(cross_queries, cross_cotangent, gate, vision_kv, block_map, self_queries, self_keys,
              self_values, self_cotangent, doc_ids):
    group_size = HEADS // KVH
    gate_total = jnp.zeros((HEADS,), jnp.float32)
    cross_list = []
    vision_list = []
    query_list = []
    key_list = []
    value_list = []
    for sequence in range(SEQS):
        span_queries = cross_queries[sequence].reshape(BLOCKS, TOK_DEV, HEADS * HD)
        span_cots = cross_cotangent[sequence].reshape(BLOCKS, TOK_DEV, HEADS * HD)
        blocks_here = vision_kv[sequence]
        earlier = jnp.roll(blocks_here, 1, axis=0)
        chosen = block_map[sequence]
        picked = jnp.where((chosen == 1)[:, None, None], earlier, blocks_here)

        def per_span(operands):
            return cross_span(operands[0], operands[1], operands[2], gate)

        query_grad, block_grad, gate_term = lax.map(per_span, (span_queries, span_cots, picked))
        is_live = chosen != 2
        query_grad = jnp.where(is_live[:, None, None], query_grad, jnp.zeros_like(query_grad))
        gate_total = gate_total + jnp.sum(jnp.where(is_live[:, None], gate_term, 0.0), axis=0)
        own_term = jnp.where((chosen == 0)[:, None, None], block_grad, 0.0)
        later_term = jnp.where((chosen == 1)[:, None, None], block_grad, 0.0)
        later_term = jnp.concatenate([later_term[1:], jnp.zeros_like(later_term[:1])], axis=0)
        cross_list.append(query_grad.reshape(TOKENS, HEADS * HD))
        vision_list.append((own_term + later_term).astype(jnp.bfloat16))

        query_heads = self_queries[sequence].reshape(TOKENS, HEADS, HD)
        key_heads = jnp.repeat(self_keys[sequence].reshape(TOKENS, KVH, HD), group_size, axis=1)
        value_heads = jnp.repeat(self_values[sequence].reshape(TOKENS, KVH, HD), group_size, axis=1)
        cot_heads = self_cotangent[sequence].reshape(TOKENS, HEADS, HD)
        query_grad, key_grad, value_grad = self_attend(query_heads, key_heads, value_heads, cot_heads,
                                                       doc_ids[sequence])
        query_list.append(query_grad.reshape(TOKENS, HEADS * HD))
        key_list.append(key_grad.reshape(TOKENS, KVH, group_size, HD).sum(axis=2).reshape(
            TOKENS, KVH * HD).astype(jnp.bfloat16))
        value_list.append(value_grad.reshape(TOKENS, KVH, group_size, HD).sum(axis=2).reshape(
            TOKENS, KVH * HD).astype(jnp.bfloat16))
    return (jnp.stack(cross_list), gate_total, jnp.stack(vision_list), jnp.stack(query_list),
            jnp.stack(key_list), jnp.stack(value_list))
```

```python
import math

import jax
import jax.numpy as jnp
from jax import lax
from jax.experimental import pallas as pl
from jax.experimental.pallas import tpu as pltpu
from jax.sharding import PartitionSpec as P

HEADS = 32
KVH = 4
HD = 128
GROUP = HEADS // KVH
VROWS = 1601
WHOLE = VROWS - 1
NK = 1616
TOK = 128
SPAN = 5
WIN = SPAN * TOK
NQ = GROUP * TOK
KVW = KVH * HD
FACTOR = HD**-0.5
EXP2 = FACTOR * math.log2(math.e)
NEG = -1e30
SUB = 16

F32 = jnp.float32
BF = jnp.bfloat16
NT = (((1,), (1,)), ((), ()))
NN = (((1,), (0,)), ((), ()))
MESH = pl.DeviceIdType.MESH


def dot(a, b, dims):
    return lax.dot_general(a, b, dims, preferred_element_type=F32)


def fold(x, op):
    total = x[0:8]
    for i in range(8, x.shape[0], 8):
        total = op(total, x[i : i + 8])
    return total


def key_phase(nk, k, q_s, c_s, tq_s, do_s, e_scr, eb, adjust, scale_row):
    scores = dot(k[...], q_s[...], NT)
    m8 = jnp.full((8, NQ), NEG, F32)
    for i in range(0, nk, SUB):
        x = adjust(i, scores[i : i + SUB])
        e_scr[pl.ds(i, SUB), :] = x
        m8 = jnp.maximum(m8, fold(x, jnp.maximum))
    m = jnp.max(m8, axis=0, keepdims=True) * EXP2
    l8 = jnp.zeros((8, NQ), F32)
    for i in range(0, nk, SUB):
        e = jnp.exp2(e_scr[pl.ds(i, SUB), :] * EXP2 - m)
        l8 = l8 + fold(e, jnp.add)
        e_scr[pl.ds(i, SUB), :] = e
        eb[pl.ds(i, SUB), :] = e.astype(BF)
    r = 1.0 / jnp.sum(l8, axis=0, keepdims=True)
    for h in range(GROUP):
        rows = slice(h * TOK, h * TOK + TOK)
        wide = jnp.broadcast_to(scale_row(h, r[:, rows]), (TOK, HD)).T
        tq_s[rows, :] = (q_s[rows, :].astype(F32) * wide).astype(BF)
        do_s[rows, :] = (c_s[rows, :].astype(F32) * wide).astype(BF)
    return r


def value_phase(nk, v, c_s, e_scr, d_scr, ds, r):
    raw = dot(v[...], c_s[...], NT)
    e8 = jnp.zeros((8, NQ), F32)
    for i in range(0, nk, SUB):
        d = raw[i : i + SUB]
        e8 = e8 + fold(e_scr[pl.ds(i, SUB), :] * d, jnp.add)
        d_scr[pl.ds(i, SUB), :] = d
    inner = jnp.sum(e8, axis=0, keepdims=True) * r
    for i in range(0, nk, SUB):
        ds[pl.ds(i, SUB), :] = (e_scr[pl.ds(i, SUB), :] * (d_scr[pl.ds(i, SUB), :] - inner)).astype(BF)
    return inner


def kernel(
    xq, xc, gate, vis, bmap, sq, sk, sv, sc, doc,
    xdq, esum, vgrad, sdq, kgrad, valgrad,
    recv, own, xq_v, xc_v, sq_v, sc_v, line, pair, dline, dpair,
    kp, vp, k_t, q_s, c_s, tq_s, do_s, e_scr, d_scr, eb, ds, bias,
    gown, gsend, garr, xdq_v, sdq_v, og, ag, bg, xs, xr, bs, br, as_, ar,
    ld_sem, own_sem, out_sem, v_ss, v_rs, h_ss, h_rs, d_ss, d_rs, g_ss, g_rs, s_ss, s_rs,
):
    count = lax.axis_size("seq")
    me = lax.axis_index("seq")
    par = lax.rem(me, 2)
    next1, prev1 = lax.rem(me + 1, count), lax.rem(me + count - 1, count)
    next2, prev2 = lax.rem(me + 2, count), lax.rem(me + count - 2, count)
    other = me + 1 - 2 * par
    bm = bmap[0, 0]

    def remote(src, dst, send, arrive, device):
        return pltpu.make_async_remote_copy(
            src_ref=src, dst_ref=dst, send_sem=send, recv_sem=arrive,
            device_id={"seq": device}, device_id_type=MESH,
        )

    barrier = pltpu.get_barrier_semaphore()
    for device in (next1, prev1, next2, prev2):
        pl.semaphore_signal(barrier, inc=1, device_id={"seq": device}, device_id_type=MESH)

    loads = [
        pltpu.make_async_copy(sk.at[0], line.at[0, 0], ld_sem.at[0]),
        pltpu.make_async_copy(sv.at[0], line.at[0, 1], ld_sem.at[1]),
        pltpu.make_async_copy(sq.at[0], sq_v, ld_sem.at[2]),
        pltpu.make_async_copy(sc.at[0], sc_v, ld_sem.at[3]),
        pltpu.make_async_copy(xq.at[0], xq_v, ld_sem.at[4]),
        pltpu.make_async_copy(xc.at[0], xc_v, ld_sem.at[5]),
    ]
    for copy in loads:
        copy.start()
    parts = []
    for h in range(KVH):
        for half in range(2):
            column = pl.ds(half * KVW + h * HD, HD)
            parts.append((2 * h + half, vis.at[0, 0, :, column]))
    for i, src in parts:
        pltpu.make_async_copy(src, own.at[i], own_sem.at[i]).start()
    dline[0] = jnp.broadcast_to(doc[...], (8, TOK))
    pl.semaphore_wait(barrier, 4)

    first = [
        remote(sk.at[0], line.at[1, 0], h_ss.at[0], h_rs.at[0], next2),
        remote(sv.at[0], line.at[1, 1], h_ss.at[1], h_rs.at[1], next2),
        remote(dline.at[0], dline.at[1], d_ss.at[0], d_rs.at[0], next2),
    ]
    for copy in (first[2], first[0], first[1]):
        copy.start()
    relay = [
        remote(line.at[1, 0], line.at[2, 0], h_ss.at[2], h_rs.at[2], next2),
        remote(line.at[1, 1], line.at[2, 1], h_ss.at[3], h_rs.at[3], next2),
        remote(dline.at[1], dline.at[2], d_ss.at[1], d_rs.at[1], next2),
    ]
    for i in (2, 0, 1):
        first[i].wait_recv()
        relay[i].start()
    for i, src in parts:
        remote(src, recv.at[i], v_ss.at[i], v_rs.at[i], next1).start()
    loads[0].wait()
    loads[1].wait()
    share = [
        remote(line.at[par], pair.at[0], h_ss.at[4], h_rs.at[4], other),
        remote(dline.at[par], dpair.at[0], d_ss.at[2], d_rs.at[2], other),
        remote(line.at[par + 1], pair.at[1], h_ss.at[5], h_rs.at[5], other),
        remote(dline.at[par + 1], dpair.at[1], d_ss.at[3], d_rs.at[3], other),
    ]
    share[0].start()
    share[1].start()
    for i in (2, 0, 1):
        relay[i].wait_recv()
    share[2].start()
    share[3].start()
    for copy in share:
        copy.wait_recv()
    for copy in loads[2:]:
        copy.wait()

    mine = dline[0, 0:1, :].astype(F32)
    lanes = lax.broadcasted_iota(jnp.int32, (TOK, TOK), 1)
    sublanes = lax.broadcasted_iota(jnp.int32, (TOK, TOK), 0)
    docs = (dline[0, 0:1, :], dpair[0, 0:1, :], dline[1, 0:1, :], dpair[1, 0:1, :], dline[2, 0:1, :])
    for back, row in enumerate(docs):
        theirs = jnp.broadcast_to(row.astype(F32), (TOK, TOK)).T
        limit = jnp.where(me >= back, TOK if back else 0, -2 * TOK)
        allowed = (theirs == mine) & (sublanes <= lanes + limit)
        bias[pl.ds(back * TOK, TOK), :] = jnp.where(allowed, 0.0, NEG)

    def gather_heads(group, queries, cots):
        for h in range(GROUP):
            rows = slice(h * TOK, h * TOK + TOK)
            column = pl.ds(pl.multiple_of(group * NQ + h * HD, HD), HD)
            q_s[rows, :] = queries[:, column]
            c_s[rows, :] = cots[:, column]

    def transposed(src, nk):
        for i in range(0, nk, TOK):
            n = min(TOK, nk - i)
            tile = src[pl.ds(i, n), :]
            if n < TOK:
                tile = jnp.concatenate([tile, jnp.zeros((TOK - n, HD), BF)], axis=0)
            k_t[:, i : i + TOK] = tile.T

    blocks = ((line, 0), (pair, 0), (line, 1), (pair, 1), (line, 2))

    def self_group(g, carry):
        column = pl.ds(pl.multiple_of(g * HD, HD), HD)
        gather_heads(g, sq_v, sc_v)
        for b, (ref, slot) in enumerate(blocks):
            rows = pl.ds(b * TOK, TOK)
            kp[rows, :] = ref[slot, 0, :, column]
            vp[rows, :] = ref[slot, 1, :, column]
        k = kp.at[pl.ds(0, WIN)]
        transposed(k, WIN)

        def adjust(i, x):
            return x + jnp.concatenate([bias[pl.ds(i, SUB), :]] * GROUP, axis=1)

        eb_w, ds_w = eb.at[pl.ds(0, WIN)], ds.at[pl.ds(0, WIN)]
        r = key_phase(WIN, k, q_s, c_s, tq_s, do_s, e_scr, eb_w, adjust, lambda h, x: x)
        value_grad = dot(eb_w[...], do_s[...], NN)
        value_phase(WIN, vp.at[pl.ds(0, WIN)], c_s, e_scr, d_scr, ds_w, r)
        key_grad = dot(ds_w[...], tq_s[...], NN) * FACTOR
        dq_t = dot(k_t[:, 0:WIN], ds_w[...], NN)
        for h in range(GROUP):
            lane = slice(h * TOK, h * TOK + TOK)
            out = pl.ds(pl.multiple_of(g * NQ + h * HD, HD), HD)
            sdq_v[:, out] = (dq_t[:, lane] * (r[:, lane] * FACTOR)).T.astype(BF)
        for half, grad in enumerate((key_grad, value_grad)):
            og[half, :, column] = grad[0:TOK]
            xs[0, half, :, column] = grad[TOK : 2 * TOK].astype(BF)
            ag[half, :, column] = grad[2 * TOK : 3 * TOK]
            xs[1, half, :, column] = grad[3 * TOK : 4 * TOK].astype(BF)
            bg[half, :, column] = grad[4 * TOK : 5 * TOK]
        return carry

    lax.fori_loop(0, KVH, self_group, 0)
    swap = remote(xs, xr, s_ss.at[0], s_rs.at[0], other)
    far = remote(bs, br, s_ss.at[1], s_rs.at[1], prev2)
    near = remote(as_, ar, s_ss.at[2], s_rs.at[2], prev2)
    swap.start()
    sdq_out = pltpu.make_async_copy(sdq_v, sdq.at[0], out_sem.at[0])
    sdq_out.start()

    def grad_copy(i):
        return remote(gsend.at[i], garr.at[i], g_ss.at[i], g_rs.at[i], prev1)

    def load_part(dst, i):
        pltpu.make_async_copy(vis.at[0, 0, :, pl.ds(0, HD)], own.at[i], own_sem.at[i]).wait()
        remote(vis.at[0, 0, :, pl.ds(0, HD)], recv.at[i], v_ss.at[i], v_rs.at[i], next1).wait_recv()
        for b in range(0, WHOLE, 320):
            rows = pl.ds(b, 320)
            dst[rows, :] = jnp.where(bm == 1, recv[i, rows, :], own[i, rows, :])
        last = jnp.where(bm == 1, recv[i, pl.ds(WHOLE, 1), :].astype(F32), own[i, pl.ds(WHOLE, 1), :].astype(F32))
        top = lax.broadcasted_iota(jnp.int32, (NK - WHOLE, HD), 0) < 1
        dst[pl.ds(WHOLE, NK - WHOLE), :] = jnp.where(top, jnp.broadcast_to(last, (NK - WHOLE, HD)), 0.0).astype(BF)

    def send_grad(i, grad):
        keep = jnp.where(bm == 0, 1.0, 0.0).astype(F32)
        give = jnp.where(bm == 1, 1.0, 0.0).astype(F32)
        for b, n in ((0, 400), (400, 400), (800, 400), (1200, 400), (WHOLE, 1)):
            part = grad[b : b + n]
            gown[i, pl.ds(b, n), :] = part * keep
            gsend[i, pl.ds(b, n), :] = (part * give).astype(BF)
        grad_copy(i).start()

    def finish_part(i):
        grad_copy(i).wait_recv()
        for b, n in ((0, 400), (400, 400), (800, 400), (1200, 400), (WHOLE, 1)):
            rows = pl.ds(b, n)
            own[i, rows, :] = (gown[i, rows, :] + garr[i, rows, :].astype(F32)).astype(BF)

    def cross_group(h, carry):
        gather_heads(h, xq_v, xc_v)
        load_part(kp, 2 * h)
        transposed(kp, NK)
        gates = [jnp.tanh(jnp.full((1, TOK), gate[h * GROUP + j], F32)) for j in range(GROUP)]
        live = jnp.where(bm == 2, 0.0, 1.0).astype(F32)

        def adjust(i, x):
            if i + SUB <= VROWS:
                return x
            return jnp.where(lax.broadcasted_iota(jnp.int32, x.shape, 0) < VROWS - i, x, NEG)

        r = key_phase(NK, kp, q_s, c_s, tq_s, do_s, e_scr, eb, adjust, lambda j, x: x * gates[j])
        send_grad(2 * h + 1, dot(eb[...], do_s[...], NN))
        load_part(vp, 2 * h + 1)
        inner = value_phase(NK, vp, c_s, e_scr, d_scr, ds, r)
        send_grad(2 * h, dot(ds[...], tq_s[...], NN) * FACTOR)
        dq_t = dot(k_t[:, 0:NK], ds[...], NN)
        for j in range(GROUP):
            lane = slice(j * TOK, j * TOK + TOK)
            out = pl.ds(pl.multiple_of(h * NQ + j * HD, HD), HD)
            xdq_v[:, out] = (dq_t[:, lane] * (r[:, lane] * gates[j] * (live * FACTOR))).T.astype(BF)
            esum[pl.ds(h * GROUP + j, 1), :] = inner[:, lane] * ((1.0 - gates[j] * gates[j]) * live)

        @pl.when(h == 0)
        def _():
            swap.wait()
            even = jnp.where(par == 0, 1.0, 0.0).astype(F32)
            odd = 1.0 - even
            for half in range(2):
                x0, x1 = xr[0, half].astype(F32), xr[1, half].astype(F32)
                og[half] = og[half] + even * x0
                ag[half] = ag[half] + (odd * x0 + even * x1)
                bs[half] = (bg[half] + odd * x1).astype(BF)
            far.start()

        @pl.when(h == 1)
        def _():
            far.wait()
            for half in range(2):
                as_[half] = (ag[half] + br[half].astype(F32)).astype(BF)
            near.start()

        return carry

    lax.fori_loop(0, KVH, cross_group, 0)
    xdq_out = pltpu.make_async_copy(xdq_v, xdq.at[0], out_sem.at[1])
    xdq_out.start()
    near.wait()
    for half, out in enumerate((kgrad, valgrad)):
        out[0] = (og[half] + ar[half].astype(F32)).astype(BF)

    def part_out(i, column):
        return pltpu.make_async_copy(own.at[i], vgrad.at[0, 0, :, pl.ds(column, HD)], own_sem.at[i])

    for h in range(KVH):
        for half in (1, 0):
            i = 2 * h + half
            finish_part(i)
            part_out(i, half * KVW + h * HD).start()
    for h in range(KVH):
        for half in (1, 0):
            part_out(2 * h + half, half * KVW + h * HD).wait()
            grad_copy(2 * h + half).wait_send()
    for i, src in parts:
        remote(src, recv.at[i], v_ss.at[i], v_rs.at[i], next1).wait_send()
    for copy in first + relay + share:
        copy.wait_send()
    sdq_out.wait()
    xdq_out.wait()


def fused(*operands):
    anywhere = pl.BlockSpec(memory_space=pl.ANY)
    vmem = pl.BlockSpec(memory_space=pltpu.VMEM)
    smem = pl.BlockSpec(memory_space=pltpu.SMEM)
    wide = (1, TOK, HEADS * HD)
    shape = jax.ShapeDtypeStruct
    dma = pltpu.SemaphoreType.DMA
    vm = pltpu.VMEM
    return pl.pallas_call(
        kernel,
        in_specs=[anywhere, anywhere, smem, anywhere, smem, anywhere, anywhere, anywhere, anywhere, vmem],
        out_specs=[anywhere, vmem, anywhere, anywhere, vmem, vmem],
        out_shape=[
            shape(wide, BF),
            shape((HEADS, TOK), F32),
            shape((1, 1, VROWS, 2 * KVW), BF),
            shape(wide, BF),
            shape((1, TOK, KVW), BF),
            shape((1, TOK, KVW), BF),
        ],
        scratch_shapes=[
            vm((2 * KVH, VROWS, HD), BF),
            vm((2 * KVH, VROWS, HD), BF),
            *[vm((TOK, HEADS * HD), BF)] * 4,
            vm((3, 2, TOK, KVW), BF),
            vm((2, 2, TOK, KVW), BF),
            vm((3, 8, TOK), jnp.int32),
            vm((2, 8, TOK), jnp.int32),
            vm((NK, HD), BF),
            vm((NK, HD), BF),
            vm((HD, 1664), BF),
            *[vm((NQ, HD), BF)] * 4,
            *[vm((NK, NQ), F32)] * 2,
            *[vm((NK, NQ), BF)] * 2,
            vm((WIN, TOK), F32),
            vm((2 * KVH, VROWS, HD), F32),
            *[vm((2 * KVH, VROWS, HD), BF)] * 2,
            *[vm((TOK, HEADS * HD), BF)] * 2,
            *[vm((2, TOK, KVW), F32)] * 3,
            *[vm((2, 2, TOK, KVW), BF)] * 2,
            *[vm((2, TOK, KVW), BF)] * 4,
            dma((6,)),
            dma((2 * KVH,)),
            dma((2,)),
            *[dma((2 * KVH,))] * 2,
            *[dma((6,))] * 2,
            *[dma((4,))] * 2,
            *[dma((2 * KVH,))] * 2,
            *[dma((3,))] * 2,
        ],
        compiler_params=pltpu.CompilerParams(
            collective_id=0, has_side_effects=True, vmem_limit_bytes=60 * 2**20
        ),
        cost_estimate=pl.CostEstimate(flops=2 * 5 * NQ * KVH * HD * (NK + WIN), bytes_accessed=14 * 2**20, transcendentals=0),
    )(*operands)


def local(*operands):
    xdq, esum, vgrad, sdq, kgrad, valgrad = fused(*operands)
    gate_grad = lax.psum(jnp.sum(esum, axis=1), ("seq", "dp"))
    return xdq, gate_grad, vgrad, sdq, kgrad, valgrad


def solution(mesh):
    rows = P("dp", "seq", None)
    block = P("dp", "seq", None, None)
    return jax.shard_map(
        local,
        mesh=mesh,
        in_specs=(rows, rows, P(), block, P("dp", "seq"), rows, rows, rows, rows, P("dp", "seq")),
        out_specs=(rows, P(), block, rows, rows, rows),
        check_vma=False,
    )
```

```python
import math

import jax
import jax.numpy as jnp
from jax import lax
from jax.experimental import pallas as pl
from jax.experimental.pallas import tpu as pltpu
from jax.sharding import PartitionSpec as P

HEADS = 32
KVH = 4
HD = 128
GROUP = HEADS // KVH
VROWS = 1601
WHOLE = VROWS - 1
NK = 1616
TOK = 128
SPAN = 5
WIN = SPAN * TOK
NQ = GROUP * TOK
KVW = KVH * HD
FACTOR = HD**-0.5
EXP2 = FACTOR * math.log2(math.e)
NEG = -1e30
SUB = 16
ROW = 8

F32 = jnp.float32
BF = jnp.bfloat16
NT = (((1,), (1,)), ((), ()))
NN = (((1,), (0,)), ((), ()))
TN = (((0,), (0,)), ((), ()))
MESH = pl.DeviceIdType.MESH


def dot(a, b, dims):
    return lax.dot_general(a, b, dims, preferred_element_type=F32)


def fold(x, op):
    total = x[0:8]
    for i in range(8, x.shape[0], 8):
        total = op(total, x[i : i + 8])
    return total


def scale_rows(sums, source, group, target):
    for h in range(GROUP):
        rows = slice(h * TOK, h * TOK + TOK)
        column = pl.ds(pl.multiple_of(group * NQ + h * HD, HD), HD)
        wide = jnp.broadcast_to(sums[:, rows], (TOK, HD)).T
        target[rows, :] = (source[:, column].astype(F32) * wide).astype(BF)


def key_phase(nk, k, q_s, e_scr, eb, adjust):
    scores = dot(k[...], q_s[...], NT)
    m8 = jnp.full((8, NQ), NEG, F32)
    for i in range(0, nk, SUB):
        x = adjust(i, scores[i : i + SUB])
        e_scr[pl.ds(i, SUB), :] = x
        m8 = jnp.maximum(m8, fold(x, jnp.maximum))
    m = jnp.max(m8, axis=0, keepdims=True) * EXP2
    l8 = jnp.zeros((8, NQ), F32)
    for i in range(0, nk, SUB):
        e = jnp.exp2(e_scr[pl.ds(i, SUB), :] * EXP2 - m)
        l8 = l8 + fold(e, jnp.add)
        e_scr[pl.ds(i, SUB), :] = e
        eb[pl.ds(i, SUB), :] = e.astype(BF)
    return 1.0 / jnp.sum(l8, axis=0, keepdims=True)


def value_phase(nk, v, c_s, e_scr, d_scr, ds, r):
    raw = dot(v[...], c_s[...], NT)
    e8 = jnp.zeros((8, NQ), F32)
    for i in range(0, nk, SUB):
        d = raw[i : i + SUB]
        e8 = e8 + fold(e_scr[pl.ds(i, SUB), :] * d, jnp.add)
        d_scr[pl.ds(i, SUB), :] = d
    inner = jnp.sum(e8, axis=0, keepdims=True) * r
    for i in range(0, nk, SUB):
        ds[pl.ds(i, SUB), :] = (e_scr[pl.ds(i, SUB), :] * (d_scr[pl.ds(i, SUB), :] - inner)).astype(BF)
    return inner


def kernel(
    xq, xc, gate, vis, bmap, sq, sk, sv, sc, doc,
    xdq, gsum, vgrad, sdq, kgrad, valgrad,
    recv, own, xq_v, xc_v, sq_v, sc_v, line, pair, dline, dpair,
    kp, vp, k_t, q_s, c_s, tq_s, do_s, scores, eb, ds, bias, r_keep, esum, across, down, along,
    gown, gsend, garr, xdq_v, sdq_v, og, ag, bg, xs, xr, bs, br, as_, ar,
    ld_sem, own_sem, out_sem, v_ss, v_rs, h_ss, h_rs, d_ss, d_rs, g_ss, g_rs, s_ss, s_rs, a_ss, a_rs, b_ss, b_rs, c_ss, c_rs,
):
    count = lax.axis_size("seq")
    me = lax.axis_index("seq")
    par = lax.rem(me, 2)
    next1, prev1 = lax.rem(me + 1, count), lax.rem(me + count - 1, count)
    next2, prev2 = lax.rem(me + 2, count), lax.rem(me + count - 2, count)
    other = me + 1 - 2 * par
    bm = bmap[0, 0]

    def remote(src, dst, send, arrive, device, axis="seq"):
        return pltpu.make_async_remote_copy(
            src_ref=src, dst_ref=dst, send_sem=send, recv_sem=arrive,
            device_id={axis: device}, device_id_type=MESH,
        )

    depth = lax.axis_size("dp")
    z = lax.axis_index("dp")
    x, y = lax.rem(me, ROW), me // ROW
    stages = (
        (across, x, ROW, "seq", [y * ROW + lax.rem(x + i, ROW) for i in range(1, ROW)], a_ss, a_rs),
        (down, y, count // ROW, "seq", [lax.rem(me + i * ROW, count) for i in range(1, count // ROW)], b_ss, b_rs),
        (along, z, depth, "dp", [lax.rem(z + i, depth) for i in range(1, depth)], c_ss, c_rs),
    )
    partners = [("seq", device) for device in (next1, prev1, next2, prev2)]
    for _, _, _, axis, devices, _, _ in stages:
        partners += [(axis, device) for device in devices]
    barrier = pltpu.get_barrier_semaphore()
    for axis, device in partners:
        pl.semaphore_signal(barrier, inc=1, device_id={axis: device}, device_id_type=MESH)

    loads = [
        pltpu.make_async_copy(sk.at[0], line.at[0, 0], ld_sem.at[0]),
        pltpu.make_async_copy(sv.at[0], line.at[0, 1], ld_sem.at[1]),
        pltpu.make_async_copy(sq.at[0], sq_v, ld_sem.at[2]),
        pltpu.make_async_copy(sc.at[0], sc_v, ld_sem.at[3]),
        pltpu.make_async_copy(xq.at[0], xq_v, ld_sem.at[4]),
        pltpu.make_async_copy(xc.at[0], xc_v, ld_sem.at[5]),
    ]
    for copy in loads:
        copy.start()
    parts = []
    for h in range(KVH):
        for half in range(2):
            column = pl.ds(half * KVW + h * HD, HD)
            parts.append((2 * h + half, vis.at[0, 0, :, column]))
    for i, src in parts:
        pltpu.make_async_copy(src, own.at[i], own_sem.at[i]).start()
    dline[0] = jnp.broadcast_to(doc[...], (8, TOK))
    esum[...] = jnp.zeros_like(esum)
    pl.semaphore_wait(barrier, len(partners))

    first = [
        remote(sk.at[0], line.at[1, 0], h_ss.at[0], h_rs.at[0], next2),
        remote(sv.at[0], line.at[1, 1], h_ss.at[1], h_rs.at[1], next2),
        remote(dline.at[0], dline.at[1], d_ss.at[0], d_rs.at[0], next2),
    ]
    relay = [
        remote(line.at[1, 0], line.at[2, 0], h_ss.at[2], h_rs.at[2], next2),
        remote(line.at[1, 1], line.at[2, 1], h_ss.at[3], h_rs.at[3], next2),
        remote(dline.at[1], dline.at[2], d_ss.at[1], d_rs.at[1], next2),
    ]
    share0 = [
        remote(line.at[par, 0], pair.at[0, 0], h_ss.at[4], h_rs.at[4], other),
        remote(line.at[par, 1], pair.at[0, 1], h_ss.at[5], h_rs.at[5], other),
        remote(dline.at[par], dpair.at[0], d_ss.at[2], d_rs.at[2], other),
    ]
    share1 = [
        remote(line.at[par + 1, 0], pair.at[1, 0], h_ss.at[6], h_rs.at[6], other),
        remote(line.at[par + 1, 1], pair.at[1, 1], h_ss.at[7], h_rs.at[7], other),
        remote(dline.at[par + 1], dpair.at[1], d_ss.at[3], d_rs.at[3], other),
    ]
    for i in (2, 0, 1):
        first[i].start()
    loads[0].wait()
    loads[1].wait()
    for i in (2, 0, 1):
        first[i].wait_recv()
        relay[i].start()
        share0[i].start()
    for i, src in parts:
        remote(src, recv.at[i], v_ss.at[i], v_rs.at[i], next1).start()
    for i in (2, 0):
        relay[i].wait_recv()
        share1[i].start()
    for i in (2, 0):
        share0[i].wait_recv()
        share1[i].wait_recv()
    for copy in loads[2:]:
        copy.wait()

    mine = dline[0, 0:1, :].astype(F32)
    lanes = lax.broadcasted_iota(jnp.int32, (TOK, TOK), 1)
    sublanes = lax.broadcasted_iota(jnp.int32, (TOK, TOK), 0)
    docs = (dline[0, 0:1, :], dpair[0, 0:1, :], dline[1, 0:1, :], dpair[1, 0:1, :], dline[2, 0:1, :])
    for back, row in enumerate(docs):
        theirs = jnp.broadcast_to(row.astype(F32), (TOK, TOK)).T
        limit = jnp.where(me >= back, TOK if back else 0, -2 * TOK)
        allowed = (theirs == mine) & (sublanes <= lanes + limit)
        bias[pl.ds(back * TOK, TOK), :] = jnp.where(allowed, 0.0, NEG)

    def gather_heads(group, source, target):
        for h in range(GROUP):
            column = pl.ds(pl.multiple_of(group * NQ + h * HD, HD), HD)
            target[h * TOK : h * TOK + TOK, :] = source[:, column]

    def transposed(src, nk):
        for i in range(0, nk, TOK):
            n = min(TOK, nk - i)
            tile = src[pl.ds(i, n), :]
            if n < TOK:
                tile = jnp.concatenate([tile, jnp.zeros((TOK - n, HD), BF)], axis=0)
            k_t[:, i : i + TOK] = tile.T

    blocks = ((line, 0), (pair, 0), (line, 1), (pair, 1), (line, 2))

    eb_w, ds_w = eb.at[pl.ds(0, WIN)], ds.at[pl.ds(0, WIN)]
    k_w, v_w = kp.at[pl.ds(0, WIN)], vp.at[pl.ds(0, WIN)]

    def window(g, half, target):
        column = pl.ds(pl.multiple_of(g * HD, HD), HD)
        for b, (ref, slot) in enumerate(blocks):
            target[pl.ds(b * TOK, TOK), :] = ref[slot, half, :, column]

    def spread(g, half, grad):
        column = pl.ds(pl.multiple_of(g * HD, HD), HD)
        og[half, :, column] = grad[0:TOK]
        xs[0, half, :, column] = grad[TOK : 2 * TOK].astype(BF)
        ag[half, :, column] = grad[2 * TOK : 3 * TOK]
        xs[1, half, :, column] = grad[3 * TOK : 4 * TOK].astype(BF)
        bg[half, :, column] = grad[4 * TOK : 5 * TOK]

    def group_scores(g):
        return scores.at[pl.ds(pl.multiple_of(g * WIN, WIN), WIN)]

    def self_keys(g, carry):
        gather_heads(g, sq_v, q_s)
        window(g, 0, k_w)

        def adjust(i, x):
            return x + jnp.concatenate([bias[pl.ds(i, SUB), :]] * GROUP, axis=1)

        r = key_phase(WIN, k_w, q_s, group_scores(g), eb_w, adjust)
        r_keep[g, 0:1, :] = r
        scale_rows(r, sc_v, g, do_s)
        spread(g, 1, dot(eb_w[...], do_s[...], NN))

        @pl.when(g == 1)
        def _():
            relay[1].wait_recv()
            share1[1].start()

        return carry

    def self_values(g, carry):
        gather_heads(g, sc_v, c_s)
        window(g, 0, k_w)
        window(g, 1, v_w)
        transposed(k_w, WIN)
        r = r_keep[g, 0:1, :]
        scale_rows(r, sq_v, g, tq_s)
        value_phase(WIN, v_w, c_s, group_scores(g), scores.at[pl.ds(KVH * WIN, WIN)], ds_w, r)
        spread(g, 0, dot(ds_w[...], tq_s[...], NN) * FACTOR)
        dq_t = dot(k_t[:, 0:WIN], ds_w[...], NN)
        for h in range(GROUP):
            lane = slice(h * TOK, h * TOK + TOK)
            out = pl.ds(pl.multiple_of(g * NQ + h * HD, HD), HD)
            sdq_v[:, out] = (dq_t[:, lane] * (r[:, lane] * FACTOR)).T.astype(BF)
        return carry

    lax.fori_loop(0, KVH, self_keys, 0)
    share0[1].wait_recv()
    share1[1].wait_recv()
    lax.fori_loop(0, KVH, self_values, 0)
    swap = remote(xs, xr, s_ss.at[0], s_rs.at[0], other)
    far = remote(bs, br, s_ss.at[1], s_rs.at[1], prev2)
    near = remote(as_, ar, s_ss.at[2], s_rs.at[2], prev2)
    swap.start()
    sdq_out = pltpu.make_async_copy(sdq_v, sdq.at[0], out_sem.at[0])
    sdq_out.start()

    def grad_copy(i):
        return remote(gsend.at[i], garr.at[i], g_ss.at[i], g_rs.at[i], prev1)

    def load_part(dst, i):
        pltpu.make_async_copy(vis.at[0, 0, :, pl.ds(0, HD)], own.at[i], own_sem.at[i]).wait()
        remote(vis.at[0, 0, :, pl.ds(0, HD)], recv.at[i], v_ss.at[i], v_rs.at[i], next1).wait_recv()
        for b in range(0, WHOLE, 320):
            rows = pl.ds(b, 320)
            dst[rows, :] = jnp.where(bm == 1, recv[i, rows, :], own[i, rows, :])
        last = jnp.where(bm == 1, recv[i, pl.ds(WHOLE, 1), :].astype(F32), own[i, pl.ds(WHOLE, 1), :].astype(F32))
        top = lax.broadcasted_iota(jnp.int32, (NK - WHOLE, HD), 0) < 1
        dst[pl.ds(WHOLE, NK - WHOLE), :] = jnp.where(top, jnp.broadcast_to(last, (NK - WHOLE, HD)), 0.0).astype(BF)

    def send_grad(i, grad):
        keep = jnp.where(bm == 0, 1.0, 0.0).astype(F32)
        give = jnp.where(bm == 1, 1.0, 0.0).astype(F32)
        for b, n in ((0, 400), (400, 400), (800, 400), (1200, 400), (WHOLE, 1)):
            part = grad[b : b + n]
            gown[i, pl.ds(b, n), :] = part * keep
            gsend[i, pl.ds(b, n), :] = (part * give).astype(BF)
        grad_copy(i).start()

    def finish_part(i):
        grad_copy(i).wait_recv()
        for b, n in ((0, 400), (400, 400), (800, 400), (1200, 400), (WHOLE, 1)):
            rows = pl.ds(b, n)
            own[i, rows, :] = (gown[i, rows, :] + garr[i, rows, :].astype(F32)).astype(BF)

    def stage_copy(number, i):
        buffer, place, size, axis, devices, send, arrive = stages[number]
        return remote(buffer.at[place], buffer.at[place], send.at[i], arrive.at[place], devices[i - 1], axis)

    def stage_start(number, value):
        buffer, place, size = stages[number][:3]
        buffer[place] = jnp.broadcast_to(value, (8, TOK))
        for i in range(1, size):
            stage_copy(number, i).start()

    def stage_end(number):
        buffer, place, size, axis, devices, send, arrive = stages[number]
        for i in range(1, size):
            source = lax.rem(place + i, size)
            remote(buffer.at[source], buffer.at[source], send.at[i], arrive.at[source], devices[i - 1], axis).wait_recv()
        total = buffer[0, 0:1, :]
        for i in range(1, size):
            total = total + buffer[i, 0:1, :]
        return total

    def part_out(h, half):
        column = pl.ds(pl.multiple_of(half * KVW + h * HD, HD), HD)
        i = 2 * h + half
        return pltpu.make_async_copy(own.at[i], vgrad.at[0, 0, :, column], own_sem.at[i])

    def done_part(h, half):
        finish_part(2 * h + half)
        part_out(h, half).start()

    def done_group(h):
        done_part(h, 1)
        done_part(h, 0)

    e_scr, d_scr = scores.at[pl.ds(0, NK)], scores.at[pl.ds(NK, NK)]

    def cross_group(h, carry):
        gather_heads(h, xq_v, q_s)
        gather_heads(h, xc_v, c_s)
        load_part(kp, 2 * h)
        transposed(kp, NK)
        gates = jnp.concatenate([jnp.tanh(jnp.full((1, TOK), gate[h * GROUP + j], F32)) for j in range(GROUP)], axis=1)
        live = jnp.where(bm == 2, 0.0, 1.0).astype(F32)

        def adjust(i, x):
            if i + SUB <= VROWS:
                return x
            return jnp.where(lax.broadcasted_iota(jnp.int32, x.shape, 0) < VROWS - i, x, NEG)

        r = key_phase(NK, kp, q_s, e_scr, eb, adjust)
        scale_rows(r * gates, xq_v, h, tq_s)
        scale_rows(r * gates, xc_v, h, do_s)
        send_grad(2 * h + 1, dot(eb[...], do_s[...], NN))
        load_part(vp, 2 * h + 1)
        inner = value_phase(NK, vp, c_s, e_scr, d_scr, ds, r)
        terms = inner * ((1.0 - gates * gates) * live)
        for j in range(GROUP):
            esum[pl.ds(h * GROUP + j, 1), :] = terms[:, j * TOK : j * TOK + TOK]

        @pl.when(h == KVH - 1)
        def _():
            stage_start(0, jnp.sum(esum[...].T, axis=0, keepdims=True))

        send_grad(2 * h, dot(ds[...], tq_s[...], NN) * FACTOR)
        dq_t = dot(k_t[:, 0:NK], ds[...], NN)
        factor = r * gates * (live * FACTOR)
        for j in range(GROUP):
            lane = slice(j * TOK, j * TOK + TOK)
            out = pl.ds(pl.multiple_of(h * NQ + j * HD, HD), HD)
            xdq_v[:, out] = (dq_t[:, lane] * factor[:, lane]).T.astype(BF)

        @pl.when(h == 0)
        def _():
            swap.wait()
            even = jnp.where(par == 0, 1.0, 0.0).astype(F32)
            odd = 1.0 - even
            for half in range(2):
                x0, x1 = xr[0, half].astype(F32), xr[1, half].astype(F32)
                og[half] = og[half] + even * x0
                ag[half] = ag[half] + (odd * x0 + even * x1)
                bs[half] = (bg[half] + odd * x1).astype(BF)
            far.start()

        @pl.when(h >= 2)
        def _():
            done_group(h - 2)

        @pl.when(h == 1)
        def _():
            far.wait()
            for half in range(2):
                as_[half] = (ag[half] + br[half].astype(F32)).astype(BF)
            near.start()

        return carry

    lax.fori_loop(0, KVH, cross_group, 0)
    xdq_out = pltpu.make_async_copy(xdq_v, xdq.at[0], out_sem.at[1])
    xdq_out.start()

    near.wait()
    for half, out in enumerate((kgrad, valgrad)):
        out[0] = (og[half] + ar[half].astype(F32)).astype(BF)

    stage_start(1, stage_end(0))
    done_part(KVH - 2, 1)
    done_part(KVH - 2, 0)
    stage_start(2, stage_end(1))
    done_part(KVH - 1, 1)
    gsum[...] = stage_end(2)
    done_part(KVH - 1, 0)
    for number, stage in enumerate(stages):
        for i in range(1, stage[2]):
            stage_copy(number, i).wait_send()
    for h in range(KVH):
        for half in (1, 0):
            part_out(h, half).wait()
            grad_copy(2 * h + half).wait_send()
    for i, src in parts:
        remote(src, recv.at[i], v_ss.at[i], v_rs.at[i], next1).wait_send()
    for copy in first + relay + share0 + share1:
        copy.wait_send()
    sdq_out.wait()
    xdq_out.wait()


def fused(*operands):
    anywhere = pl.BlockSpec(memory_space=pl.ANY)
    vmem = pl.BlockSpec(memory_space=pltpu.VMEM)
    smem = pl.BlockSpec(memory_space=pltpu.SMEM)
    wide = (1, TOK, HEADS * HD)
    shape = jax.ShapeDtypeStruct
    dma = pltpu.SemaphoreType.DMA
    vm = pltpu.VMEM
    return pl.pallas_call(
        kernel,
        in_specs=[anywhere, anywhere, smem, anywhere, smem, anywhere, anywhere, anywhere, anywhere, vmem],
        out_specs=[anywhere, vmem, anywhere, anywhere, vmem, vmem],
        out_shape=[
            shape(wide, BF),
            shape((1, TOK), F32),
            shape((1, 1, VROWS, 2 * KVW), BF),
            shape(wide, BF),
            shape((1, TOK, KVW), BF),
            shape((1, TOK, KVW), BF),
        ],
        scratch_shapes=[
            vm((2 * KVH, VROWS, HD), BF),
            vm((2 * KVH, VROWS, HD), BF),
            *[vm((TOK, HEADS * HD), BF)] * 4,
            vm((3, 2, TOK, KVW), BF),
            vm((2, 2, TOK, KVW), BF),
            vm((3, 8, TOK), jnp.int32),
            vm((2, 8, TOK), jnp.int32),
            vm((NK, HD), BF),
            vm((NK, HD), BF),
            vm((HD, 1664), BF),
            *[vm((NQ, HD), BF)] * 4,
            vm((2 * NK, NQ), F32),
            *[vm((NK, NQ), BF)] * 2,
            vm((WIN, TOK), F32),
            vm((KVH, 8, NQ), F32),
            vm((TOK, TOK), F32),
            *[vm((8, 8, TOK), F32)] * 3,
            vm((2 * KVH, VROWS, HD), F32),
            *[vm((2 * KVH, VROWS, HD), BF)] * 2,
            *[vm((TOK, HEADS * HD), BF)] * 2,
            *[vm((2, TOK, KVW), F32)] * 3,
            *[vm((2, 2, TOK, KVW), BF)] * 2,
            *[vm((2, TOK, KVW), BF)] * 4,
            dma((6,)),
            dma((2 * KVH,)),
            dma((2,)),
            *[dma((2 * KVH,))] * 2,
            *[dma((8,))] * 2,
            *[dma((4,))] * 2,
            *[dma((2 * KVH,))] * 2,
            *[dma((3,))] * 2,
            *[dma((8,))] * 6,
        ],
        compiler_params=pltpu.CompilerParams(
            collective_id=0, has_side_effects=True, vmem_limit_bytes=60 * 2**20
        ),
        cost_estimate=pl.CostEstimate(flops=2 * 5 * NQ * KVH * HD * (NK + WIN), bytes_accessed=14 * 2**20, transcendentals=0),
    )(*operands)


def settle_kernel(*refs):
    half = len(refs) // 2
    for src, dst in zip(refs[:half], refs[half:]):
        dst[...] = src[...]


def settle(xdq, vgrad, sdq, kgrad, valgrad):
    steps = 8
    rows = TOK // steps
    wide = pl.BlockSpec((1, rows, HEADS * HD), lambda i: (0, i, 0))
    image = pl.BlockSpec((1, 1, 208, 2 * KVW), lambda i: (0, 0, i, 0))
    narrow = pl.BlockSpec((1, rows, KVW), lambda i: (0, i, 0))
    arrays = (xdq, vgrad, sdq, kgrad, valgrad)
    specs = [wide, image, wide, narrow, narrow]
    return pl.pallas_call(
        settle_kernel,
        grid=(steps,),
        in_specs=specs,
        out_specs=specs,
        out_shape=[jax.ShapeDtypeStruct(x.shape, x.dtype) for x in arrays],
    )(*arrays)


def local(*operands):
    xdq, gsum, vgrad, sdq, kgrad, valgrad = fused(*operands)
    xdq, vgrad, sdq, kgrad, valgrad = settle(xdq, vgrad, sdq, kgrad, valgrad)
    return xdq, gsum[0, :HEADS], vgrad, sdq, kgrad, valgrad


def solution(mesh):
    rows = P("dp", "seq", None)
    block = P("dp", "seq", None, None)
    return jax.shard_map(
        local,
        mesh=mesh,
        in_specs=(rows, rows, P(), block, P("dp", "seq"), rows, rows, rows, rows, P("dp", "seq")),
        out_specs=(rows, P(), block, rows, rows, rows),
        check_vma=False,
    )
```

```python
import math

import jax
import jax.numpy as jnp
from jax import lax
from jax.experimental import pallas as pl
from jax.experimental.pallas import tpu as pltpu
from jax.sharding import PartitionSpec as P

HEADS = 32
KVH = 4
HD = 128
GROUP = HEADS // KVH
VROWS = 1601
WHOLE = VROWS - 1
NK = 1616
TOK = 128
SPAN = 5
WIN = SPAN * TOK
NQ = GROUP * TOK
KVW = KVH * HD
FACTOR = HD**-0.5
EXP2 = FACTOR * math.log2(math.e)
NEG = -1e30
SUB = 16
ROW = 8

F32 = jnp.float32
BF = jnp.bfloat16
NT = (((1,), (1,)), ((), ()))
NN = (((1,), (0,)), ((), ()))
TN = (((0,), (0,)), ((), ()))
MESH = pl.DeviceIdType.MESH


def dot(a, b, dims):
    return lax.dot_general(a, b, dims, preferred_element_type=F32)


def fold(x, op):
    total = x[0:8]
    for i in range(8, x.shape[0], 8):
        total = op(total, x[i : i + 8])
    return total


def scale_rows(sums, source, group, target):
    for h in range(GROUP):
        rows = slice(h * TOK, h * TOK + TOK)
        column = pl.ds(pl.multiple_of(group * NQ + h * HD, HD), HD)
        wide = jnp.broadcast_to(sums[:, rows], (TOK, HD)).T
        target[rows, :] = (source[:, column].astype(F32) * wide).astype(BF)


def key_phase(nk, k, q_s, e_scr, eb, adjust):
    scores = dot(k[...], q_s[...], NT)
    m8 = jnp.full((8, NQ), NEG, F32)
    for i in range(0, nk, SUB):
        x = adjust(i, scores[i : i + SUB])
        e_scr[pl.ds(i, SUB), :] = x
        m8 = jnp.maximum(m8, fold(x, jnp.maximum))
    m = jnp.max(m8, axis=0, keepdims=True) * EXP2
    l8 = jnp.zeros((8, NQ), F32)
    for i in range(0, nk, SUB):
        e = jnp.exp2(e_scr[pl.ds(i, SUB), :] * EXP2 - m)
        l8 = l8 + fold(e, jnp.add)
        e_scr[pl.ds(i, SUB), :] = e
        eb[pl.ds(i, SUB), :] = e.astype(BF)
    return 1.0 / jnp.sum(l8, axis=0, keepdims=True)


def value_phase(nk, v, c_s, e_scr, d_scr, ds, r):
    raw = dot(v[...], c_s[...], NT)
    e8 = jnp.zeros((8, NQ), F32)
    for i in range(0, nk, SUB):
        d = raw[i : i + SUB]
        e8 = e8 + fold(e_scr[pl.ds(i, SUB), :] * d, jnp.add)
        d_scr[pl.ds(i, SUB), :] = d
    inner = jnp.sum(e8, axis=0, keepdims=True) * r
    for i in range(0, nk, SUB):
        ds[pl.ds(i, SUB), :] = (e_scr[pl.ds(i, SUB), :] * (d_scr[pl.ds(i, SUB), :] - inner)).astype(BF)
    return inner


def kernel(
    xq, xc, gate, vis, bmap, sq, sk, sv, sc, doc,
    xdq_v, gsum, vgrad, sdq_v, kgrad, valgrad,
    recv, own, xq_v, xc_v, sq_v, sc_v, line, pair, dline, dpair,
    kp, vp, k_t, q_s, c_s, tq_s, do_s, scores, eb, ds, bias, r_keep, esum, across, down, along,
    gown, gsend, garr, og, ag, bg, xs, xr, bs, br, as_, ar,
    ld_sem, own_sem, v_ss, v_rs, h_ss, h_rs, d_ss, d_rs, g_ss, g_rs, s_ss, s_rs, a_ss, a_rs, b_ss, b_rs, c_ss, c_rs,
):
    count = lax.axis_size("seq")
    me = lax.axis_index("seq")
    par = lax.rem(me, 2)
    next1, prev1 = lax.rem(me + 1, count), lax.rem(me + count - 1, count)
    next2, prev2 = lax.rem(me + 2, count), lax.rem(me + count - 2, count)
    next4, prev4 = lax.rem(me + 4, count), lax.rem(me + count - 4, count)
    other = me + 1 - 2 * par
    bm = bmap[0, 0]

    def remote(src, dst, send, arrive, device, axis="seq"):
        return pltpu.make_async_remote_copy(
            src_ref=src, dst_ref=dst, send_sem=send, recv_sem=arrive,
            device_id={axis: device}, device_id_type=MESH,
        )

    depth = lax.axis_size("dp")
    z = lax.axis_index("dp")
    x, y = lax.rem(me, ROW), me // ROW
    stages = (
        (across, x, ROW, "seq", [y * ROW + lax.rem(x + i, ROW) for i in range(1, ROW)], a_ss, a_rs),
        (down, y, count // ROW, "seq", [lax.rem(me + i * ROW, count) for i in range(1, count // ROW)], b_ss, b_rs),
        (along, z, depth, "dp", [lax.rem(z + i, depth) for i in range(1, depth)], c_ss, c_rs),
    )
    partners = [("seq", device) for device in (next1, prev1, next2, prev2, next4, prev4)]
    for _, _, _, axis, devices, _, _ in stages:
        partners += [(axis, device) for device in devices]
    barrier = pltpu.get_barrier_semaphore()
    for axis, device in partners:
        pl.semaphore_signal(barrier, inc=1, device_id={axis: device}, device_id_type=MESH)

    loads = [
        pltpu.make_async_copy(sk.at[0], line.at[0, 0], ld_sem.at[0]),
        pltpu.make_async_copy(sv.at[0], line.at[0, 1], ld_sem.at[1]),
        pltpu.make_async_copy(sq.at[0], sq_v, ld_sem.at[2]),
        pltpu.make_async_copy(sc.at[0], sc_v, ld_sem.at[3]),
        pltpu.make_async_copy(xq.at[0], xq_v, ld_sem.at[4]),
        pltpu.make_async_copy(xc.at[0], xc_v, ld_sem.at[5]),
    ]
    for copy in loads:
        copy.start()
    parts = []
    for h in range(KVH):
        for half in range(2):
            column = pl.ds(half * KVW + h * HD, HD)
            parts.append((2 * h + half, vis.at[0, 0, :, column]))
    for i, src in parts:
        pltpu.make_async_copy(src, own.at[i], own_sem.at[i]).start()
    dline[0] = jnp.broadcast_to(doc[...], (8, TOK))
    esum[...] = jnp.zeros_like(esum)
    pl.semaphore_wait(barrier, len(partners))

    first = [
        remote(sk.at[0], line.at[1, 0], h_ss.at[0], h_rs.at[0], next2),
        remote(sv.at[0], line.at[1, 1], h_ss.at[1], h_rs.at[1], next2),
        remote(dline.at[0], dline.at[1], d_ss.at[0], d_rs.at[0], next2),
    ]
    relay = [
        remote(sk.at[0], line.at[2, 0], h_ss.at[2], h_rs.at[2], next4),
        remote(sv.at[0], line.at[2, 1], h_ss.at[3], h_rs.at[3], next4),
        remote(dline.at[0], dline.at[2], d_ss.at[1], d_rs.at[1], next4),
    ]
    share0 = [
        remote(line.at[par, 0], pair.at[0, 0], h_ss.at[4], h_rs.at[4], other),
        remote(line.at[par, 1], pair.at[0, 1], h_ss.at[5], h_rs.at[5], other),
        remote(dline.at[par], dpair.at[0], d_ss.at[2], d_rs.at[2], other),
    ]
    share1 = [
        remote(line.at[par + 1, 0], pair.at[1, 0], h_ss.at[6], h_rs.at[6], other),
        remote(line.at[par + 1, 1], pair.at[1, 1], h_ss.at[7], h_rs.at[7], other),
        remote(dline.at[par + 1], dpair.at[1], d_ss.at[3], d_rs.at[3], other),
    ]
    for i in (2, 0, 1):
        first[i].start()
        relay[i].start()
    for i, src in parts:
        remote(src, recv.at[i], v_ss.at[i], v_rs.at[i], next1).start()
    loads[0].wait()
    loads[1].wait()
    for i in (2, 0):
        first[i].wait_recv()
        share0[i].start()
    for i in (2, 0):
        relay[i].wait_recv()
        share1[i].start()
    for i in (2, 0):
        share0[i].wait_recv()
        share1[i].wait_recv()
    loads[2].wait()
    loads[3].wait()

    mine = dline[0, 0:1, :].astype(F32)
    lanes = lax.broadcasted_iota(jnp.int32, (TOK, TOK), 1)
    sublanes = lax.broadcasted_iota(jnp.int32, (TOK, TOK), 0)
    docs = (dline[0, 0:1, :], dpair[0, 0:1, :], dline[1, 0:1, :], dpair[1, 0:1, :], dline[2, 0:1, :])
    for back, row in enumerate(docs):
        theirs = jnp.broadcast_to(row.astype(F32), (TOK, TOK)).T
        limit = jnp.where(me >= back, TOK if back else 0, -2 * TOK)
        allowed = (theirs == mine) & (sublanes <= lanes + limit)
        bias[pl.ds(back * TOK, TOK), :] = jnp.where(allowed, 0.0, NEG)

    def gather_heads(group, source, target):
        for h in range(GROUP):
            column = pl.ds(pl.multiple_of(group * NQ + h * HD, HD), HD)
            target[h * TOK : h * TOK + TOK, :] = source[:, column]

    def transposed(src, nk):
        for i in range(0, nk, TOK):
            n = min(TOK, nk - i)
            tile = src[pl.ds(i, n), :]
            if n < TOK:
                tile = jnp.concatenate([tile, jnp.zeros((TOK - n, HD), BF)], axis=0)
            k_t[:, i : i + TOK] = tile.T

    blocks = ((line, 0), (pair, 0), (line, 1), (pair, 1), (line, 2))

    eb_w, ds_w = eb.at[pl.ds(0, WIN)], ds.at[pl.ds(0, WIN)]
    k_w, v_w = kp.at[pl.ds(0, WIN)], vp.at[pl.ds(0, WIN)]

    def window(g, half, target):
        column = pl.ds(pl.multiple_of(g * HD, HD), HD)
        for b, (ref, slot) in enumerate(blocks):
            target[pl.ds(b * TOK, TOK), :] = ref[slot, half, :, column]

    def spread(g, half, grad):
        column = pl.ds(pl.multiple_of(g * HD, HD), HD)
        og[half, :, column] = grad[0:TOK]
        xs[0, half, :, column] = grad[TOK : 2 * TOK].astype(BF)
        ag[half, :, column] = grad[2 * TOK : 3 * TOK]
        xs[1, half, :, column] = grad[3 * TOK : 4 * TOK].astype(BF)
        bg[half, :, column] = grad[4 * TOK : 5 * TOK]

    def group_scores(g):
        return scores.at[pl.ds(pl.multiple_of(g * WIN, WIN), WIN)]

    def self_keys(g, carry):
        gather_heads(g, sq_v, q_s)
        window(g, 0, k_w)

        def adjust(i, x):
            return x + jnp.concatenate([bias[pl.ds(i, SUB), :]] * GROUP, axis=1)

        r = key_phase(WIN, k_w, q_s, group_scores(g), eb_w, adjust)
        r_keep[g, 0:1, :] = r
        scale_rows(r, sc_v, g, do_s)
        spread(g, 1, dot(eb_w[...], do_s[...], NN))

        @pl.when(g == 0)
        def _():
            first[1].wait_recv()
            share0[1].start()

        @pl.when(g == 1)
        def _():
            relay[1].wait_recv()
            share1[1].start()

        return carry

    def self_values(g, carry):
        gather_heads(g, sc_v, c_s)
        window(g, 0, k_w)
        window(g, 1, v_w)
        transposed(k_w, WIN)
        r = r_keep[g, 0:1, :]
        scale_rows(r, sq_v, g, tq_s)
        value_phase(WIN, v_w, c_s, group_scores(g), scores.at[pl.ds(KVH * WIN, WIN)], ds_w, r)
        spread(g, 0, dot(ds_w[...], tq_s[...], NN) * FACTOR)
        dq_t = dot(k_t[:, 0:WIN], ds_w[...], NN)
        for h in range(GROUP):
            lane = slice(h * TOK, h * TOK + TOK)
            out = pl.ds(pl.multiple_of(g * NQ + h * HD, HD), HD)
            sdq_v[:, out] = (dq_t[:, lane] * (r[:, lane] * FACTOR)).T.astype(BF)
        return carry

    lax.fori_loop(0, KVH, self_keys, 0)
    share0[1].wait_recv()
    share1[1].wait_recv()
    lax.fori_loop(0, KVH, self_values, 0)
    swap = remote(xs, xr, s_ss.at[0], s_rs.at[0], other)
    far = remote(bs, br, s_ss.at[1], s_rs.at[1], prev4)
    near = remote(as_, ar, s_ss.at[2], s_rs.at[2], prev2)
    swap.start()

    def grad_copy(i):
        return remote(gsend.at[i], garr.at[i], g_ss.at[i], g_rs.at[i], prev1)

    def load_part(dst, i):
        pltpu.make_async_copy(vis.at[0, 0, :, pl.ds(0, HD)], own.at[i], own_sem.at[i]).wait()
        remote(vis.at[0, 0, :, pl.ds(0, HD)], recv.at[i], v_ss.at[i], v_rs.at[i], next1).wait_recv()
        for b in range(0, WHOLE, 320):
            rows = pl.ds(b, 320)
            dst[rows, :] = jnp.where(bm == 1, recv[i, rows, :], own[i, rows, :])
        last = jnp.where(bm == 1, recv[i, pl.ds(WHOLE, 1), :].astype(F32), own[i, pl.ds(WHOLE, 1), :].astype(F32))
        top = lax.broadcasted_iota(jnp.int32, (NK - WHOLE, HD), 0) < 1
        dst[pl.ds(WHOLE, NK - WHOLE), :] = jnp.where(top, jnp.broadcast_to(last, (NK - WHOLE, HD)), 0.0).astype(BF)

    def send_grad(i, grad):
        keep = jnp.where(bm == 0, 1.0, 0.0).astype(F32)
        give = jnp.where(bm == 1, 1.0, 0.0).astype(F32)
        for b, n in ((0, 400), (400, 400), (800, 400), (1200, 400), (WHOLE, 1)):
            part = grad[b : b + n]
            gown[i, pl.ds(b, n), :] = part * keep
            gsend[i, pl.ds(b, n), :] = (part * give).astype(BF)
        grad_copy(i).start()

    def done_part(h, half):
        i = 2 * h + half
        column = pl.ds(pl.multiple_of(half * KVW + h * HD, HD), HD)
        grad_copy(i).wait_recv()
        for b, n in ((0, 400), (400, 400), (800, 400), (1200, 400), (WHOLE, 1)):
            rows = pl.ds(b, n)
            vgrad[rows, column] = (gown[i, rows, :] + garr[i, rows, :].astype(F32)).astype(BF)

    def done_group(h):
        done_part(h, 1)
        done_part(h, 0)

    def stage_copy(number, i):
        buffer, place, size, axis, devices, send, arrive = stages[number]
        return remote(buffer.at[place], buffer.at[place], send.at[i], arrive.at[place], devices[i - 1], axis)

    def stage_start(number, value):
        buffer, place, size = stages[number][:3]
        buffer[place] = jnp.broadcast_to(value, (8, TOK))
        for i in range(1, size):
            stage_copy(number, i).start()

    def stage_end(number):
        buffer, place, size, axis, devices, send, arrive = stages[number]
        for i in range(1, size):
            source = lax.rem(place + i, size)
            remote(buffer.at[source], buffer.at[source], send.at[i], arrive.at[source], devices[i - 1], axis).wait_recv()
        total = buffer[0, 0:1, :]
        for i in range(1, size):
            total = total + buffer[i, 0:1, :]
        return total

    e_scr, d_scr = scores.at[pl.ds(0, NK)], scores.at[pl.ds(NK, NK)]

    def cross_group(h, carry):
        gather_heads(h, xq_v, q_s)
        gather_heads(h, xc_v, c_s)
        load_part(kp, 2 * h)
        transposed(kp, NK)
        gates = jnp.concatenate([jnp.tanh(jnp.full((1, TOK), gate[h * GROUP + j], F32)) for j in range(GROUP)], axis=1)
        live = jnp.where(bm == 2, 0.0, 1.0).astype(F32)

        def adjust(i, x):
            if i + SUB <= VROWS:
                return x
            return jnp.where(lax.broadcasted_iota(jnp.int32, x.shape, 0) < VROWS - i, x, NEG)

        r = key_phase(NK, kp, q_s, e_scr, eb, adjust)
        scale_rows(r * gates, xq_v, h, tq_s)
        scale_rows(r * gates, xc_v, h, do_s)
        send_grad(2 * h + 1, dot(eb[...], do_s[...], NN))
        load_part(vp, 2 * h + 1)
        inner = value_phase(NK, vp, c_s, e_scr, d_scr, ds, r)
        terms = inner * ((1.0 - gates * gates) * live)
        for j in range(GROUP):
            esum[pl.ds(h * GROUP + j, 1), :] = terms[:, j * TOK : j * TOK + TOK]

        @pl.when(h == KVH - 1)
        def _():
            stage_start(0, jnp.sum(esum[...].T, axis=0, keepdims=True))

        send_grad(2 * h, dot(ds[...], tq_s[...], NN) * FACTOR)
        dq_t = dot(k_t[:, 0:NK], ds[...], NN)
        factor = r * gates * (live * FACTOR)
        for j in range(GROUP):
            lane = slice(j * TOK, j * TOK + TOK)
            out = pl.ds(pl.multiple_of(h * NQ + j * HD, HD), HD)
            xdq_v[:, out] = (dq_t[:, lane] * factor[:, lane]).T.astype(BF)

        @pl.when(h == 0)
        def _():
            swap.wait()
            even = jnp.where(par == 0, 1.0, 0.0).astype(F32)
            odd = 1.0 - even
            for half in range(2):
                x0, x1 = xr[0, half].astype(F32), xr[1, half].astype(F32)
                og[half] = og[half] + even * x0
                as_[half] = (ag[half] + (odd * x0 + even * x1)).astype(BF)
                bs[half] = (bg[half] + odd * x1).astype(BF)
            far.start()
            near.start()

        @pl.when(h >= 2)
        def _():
            done_group(h - 2)

        return carry

    loads[4].wait()
    loads[5].wait()
    lax.fori_loop(0, KVH, cross_group, 0)

    near.wait()
    far.wait()
    for half, out in enumerate((kgrad, valgrad)):
        out[...] = (og[half] + (ar[half].astype(F32) + br[half].astype(F32))).astype(BF)

    stage_start(1, stage_end(0))
    done_part(KVH - 2, 1)
    done_part(KVH - 2, 0)
    stage_start(2, stage_end(1))
    done_part(KVH - 1, 1)
    gsum[...] = stage_end(2)
    done_part(KVH - 1, 0)
    for number, stage in enumerate(stages):
        for i in range(1, stage[2]):
            stage_copy(number, i).wait_send()
    for h in range(KVH):
        for half in (1, 0):
            grad_copy(2 * h + half).wait_send()
    for i, src in parts:
        remote(src, recv.at[i], v_ss.at[i], v_rs.at[i], next1).wait_send()
    for copy in first + relay + share0 + share1:
        copy.wait_send()


def fused(*operands):
    anywhere = pl.BlockSpec(memory_space=pl.ANY)
    vmem = pl.BlockSpec(memory_space=pltpu.VMEM)
    smem = pl.BlockSpec(memory_space=pltpu.SMEM)
    shape = jax.ShapeDtypeStruct
    dma = pltpu.SemaphoreType.DMA
    vm = pltpu.VMEM
    return pl.pallas_call(
        kernel,
        in_specs=[anywhere, anywhere, smem, anywhere, smem, anywhere, anywhere, anywhere, anywhere, vmem],
        out_specs=[vmem] * 6,
        out_shape=[
            vm((TOK, HEADS * HD), BF),
            shape((1, TOK), F32),
            vm((VROWS, 2 * KVW), BF),
            vm((TOK, HEADS * HD), BF),
            vm((TOK, KVW), BF),
            vm((TOK, KVW), BF),
        ],
        scratch_shapes=[
            vm((2 * KVH, VROWS, HD), BF),
            vm((2 * KVH, VROWS, HD), BF),
            *[vm((TOK, HEADS * HD), BF)] * 4,
            vm((3, 2, TOK, KVW), BF),
            vm((2, 2, TOK, KVW), BF),
            vm((3, 8, TOK), jnp.int32),
            vm((2, 8, TOK), jnp.int32),
            vm((NK, HD), BF),
            vm((NK, HD), BF),
            vm((HD, 1664), BF),
            *[vm((NQ, HD), BF)] * 4,
            vm((2 * NK, NQ), F32),
            *[vm((NK, NQ), BF)] * 2,
            vm((WIN, TOK), F32),
            vm((KVH, 8, NQ), F32),
            vm((TOK, TOK), F32),
            *[vm((8, 8, TOK), F32)] * 3,
            vm((2 * KVH, VROWS, HD), F32),
            *[vm((2 * KVH, VROWS, HD), BF)] * 2,
            *[vm((2, TOK, KVW), F32)] * 3,
            *[vm((2, 2, TOK, KVW), BF)] * 2,
            *[vm((2, TOK, KVW), BF)] * 4,
            dma((6,)),
            dma((2 * KVH,)),
            *[dma((2 * KVH,))] * 2,
            *[dma((8,))] * 2,
            *[dma((4,))] * 2,
            *[dma((2 * KVH,))] * 2,
            *[dma((3,))] * 2,
            *[dma((8,))] * 6,
        ],
        compiler_params=pltpu.CompilerParams(
            collective_id=0, has_side_effects=True, vmem_limit_bytes=54 * 2**20
        ),
        cost_estimate=pl.CostEstimate(flops=2 * 5 * NQ * KVH * HD * (NK + WIN), bytes_accessed=14 * 2**20, transcendentals=0),
    )(*operands)


def settle_kernel(*refs):
    *refs, sem = refs
    half = len(refs) // 2
    copies = []
    for i, (src, dst) in enumerate(zip(refs[:half], refs[half:])):
        copies.append(pltpu.make_async_copy(src, dst.at[(0,) * (len(dst.shape) - 2)], sem.at[i]))
    for copy in copies:
        copy.start()
    for copy in copies:
        copy.wait()


def settle(*arrays):
    shapes = [(1,) * (2 if x.shape[0] == VROWS else 1) + x.shape for x in arrays]
    return pl.pallas_call(
        settle_kernel,
        in_specs=[pl.BlockSpec(memory_space=pltpu.VMEM)] * len(arrays),
        out_specs=[pl.BlockSpec(memory_space=pl.ANY)] * len(arrays),
        out_shape=[jax.ShapeDtypeStruct(x, BF) for x in shapes],
        scratch_shapes=[pltpu.SemaphoreType.DMA((len(arrays),))],
        compiler_params=pltpu.CompilerParams(vmem_limit_bytes=2**20),
    )(*arrays)


def local(*operands):
    xdq, gsum, vgrad, sdq, kgrad, valgrad = fused(*operands)
    xdq, vgrad, sdq, kgrad, valgrad = settle(xdq, vgrad, sdq, kgrad, valgrad)
    return xdq, gsum[0, :HEADS], vgrad, sdq, kgrad, valgrad


def solution(mesh):
    rows = P("dp", "seq", None)
    block = P("dp", "seq", None, None)
    return jax.shard_map(
        local,
        mesh=mesh,
        in_specs=(rows, rows, P(), block, P("dp", "seq"), rows, rows, rows, rows, P("dp", "seq")),
        out_specs=(rows, P(), block, rows, rows, rows),
        check_vma=False,
    )
```
